128 devices in a mesh: row: 8 (over y, x_lo), col: 16 (over z, x_hi, core).
Axes of the slice: x: 4 (x_hi: 2, x_lo: 2; x = x_hi * 2 + x_lo), y: 4, z: 4, core: 2. Of those that a mesh axis runs over, the one named last changes fastest.
Arguments:
- tokens: bfloat16 [16384, 3584], P(('row', 'col')), may hold values from -6 to 6
- expert_ids: int32 [16384, 4], P(('row', 'col')), may hold values from 0 to 127, all different within a row; in each aligned block of 128 rows (0 to 127, 128 to 255, ...) at most 5 rows name the same one
- combine_weights: float32 [16384, 4], P(('row', 'col')), may hold values from 0.1 to 1
- expert_gate: bfloat16 [128, 3584, 1024], P(('row', 'col')), may hold values from -0.09375 to 0.09375
- expert_up: bfloat16 [128, 3584, 1024], P(('row', 'col')), may hold values from -0.09375 to 0.09375
- expert_down: bfloat16 [128, 1024, 3584], P(('row', 'col')), may hold values from -0.1875 to 0.1875
- shared_gate: bfloat16 [3584, 1024], P(None, 'row'), may hold values from -0.09375 to 0.09375
- shared_up: bfloat16 [3584, 1024], P(None, 'row'), may hold values from -0.09375 to 0.09375
- shared_down: bfloat16 [1024, 3584], P('row'), may hold values from -0.1875 to 0.1875
Outputs:
- mixed: bfloat16 [16384, 3584], P(('row', 'col'))
The draws below stay inside these ranges and needn't reach their ends.
Inputs may be any that keep to these rules, and one draw needn't show every extreme that they name: `expert_ids`: each row names 4 different experts. Among the 128 rows of one device no expert is named by more than 5 rows, and in every draw some expert is named by exactly 5 rows of some device.
All inputs are finite; a program needn't handle non-finite values.
Results may differ from the reference program's by a relative error of at most 0.0055.
Values may be sent and summed in bfloat16 or wider, within the bound.
A program may use at most 128 MiB of HBM per device.

```python
import math
import jax
import jax.numpy as jnp
import numpy as np
from jax import lax

D = 3584
FF = 1024
SFF = 1024
TOP = 4
TOK_DEV = 128
EXPERTS = 128
TOKENS = 16384
CAP = 5
N_ROW = 8
N_COL = 16


def shard_levels(own_key, extent, split, smallest, high):
    factor_of = 1.0
    for position, blocks in split:
        heights = jax.random.uniform(jax.random.fold_in(jax.random.fold_in(own_key, 6), position), (blocks,), jnp.float32, smallest / len(split), high / len(split))
        factor_of = factor_of * jnp.repeat(jnp.exp(heights), extent[position] // blocks).reshape((-1,) + (1,) * (len(extent) - 1 - position))
    return factor_of


def routed_block(rng, own, number, rows, amount, top, most, slope):
    ranking = jax.random.permutation(rng, amount)
    heavy_load, ordinary = portions_of(amount, rows * top, most, slope, True), portions_of(amount, rows * top, most, slope, False)
    places = jnp.arange(amount)

    def named(lengths, rotation):
        used = int((lengths > 0).sum())
        fixed = max(1, used // 4)
        passed = fixed + (places - fixed + rotation * (used - fixed)) % max(1, amount - fixed)
        return jnp.zeros((amount,), jnp.int32).at[ranking[jnp.where(places < fixed, places, passed)]].set(jnp.asarray(lengths, jnp.int32))

    lengths = jnp.where(number % 4 == 0, named(heavy_load, number // 4), named(ordinary, number - number // 4 - 1))
    mixed = jax.random.permutation(jax.random.fold_in(own, 3), amount)
    source_of, sink = mixed[0:amount // 2 * 2:2], mixed[1:amount // 2 * 2:2]
    room = jnp.minimum(lengths[source_of] - 1, most - lengths[sink]) // 2
    room = jnp.where((source_of == ranking[0]) | (sink == ranking[0]) | (lengths[sink] == 0), 0, jnp.maximum(room, 0))
    passed = jax.random.randint(jax.random.fold_in(own, 4), (amount // 2,), 0, 1 << 20) % (room + 1)
    lengths = lengths.at[source_of].add(-passed).at[sink].add(passed)
    members = jnp.searchsorted(jnp.cumsum(lengths), jnp.arange(rows * top), side="right").astype(jnp.int32)
    listing = members.reshape(top, rows).T
    listing = listing[jax.random.permutation(jax.random.fold_in(own, 1), rows)]
    rotation = jax.random.randint(jax.random.fold_in(own, 2), (rows, 1), 0, top)
    return jnp.take_along_axis(listing, (jnp.arange(top)[None, :] + rotation) % top, axis=1)


def portions_of(number_of, total, bound, lean, full):
    portions = [(1 << 20) // math.isqrt(grade ** lean) + 1 for grade in range(1, number_of + 1)]
    largest = bound if full else min(bound, max(-(-total // number_of), total * portions[0] // sum(portions)))
    least = 1 if total - largest >= number_of - 1 else 0
    holding, spare = [largest] + [least] * (number_of - 1), total - largest - least * (number_of - 1)
    while spare > 0:
        free = [i for i in range(1, number_of) if holding[i] < largest] or [i for i in range(1, number_of) if holding[i] < bound]
        whole, budget = sum([portions[i] for i in free]), spare
        for i in free:
            addition = min(bound - holding[i], max(1, budget * portions[i] // whole), spare)
            holding[i] = holding[i] + addition
            spare = spare - addition
    return np.array(holding)


def noise(stream_key, dims, deviation, bound, cuts=(), kind=jnp.bfloat16):
    drawn = jax.random.normal(stream_key, dims, jnp.float32) * deviation
    if len(cuts) > 0:
        drawn = shard_levels(stream_key, dims, cuts, -0.22, 0.18) * drawn
    return jnp.clip(drawn, min=-bound, max=bound).astype(kind)


def setup_inputs(seed: int = 0) -> dict:
    streams_of = jax.random.split(jax.random.key(seed), 10)
    tokens = noise(streams_of[0], (TOKENS, D), 1.0, 6.0, ((0, 128),))
    expert_ids_keys = jax.random.split(jax.random.fold_in(streams_of[1], 1), TOKENS // TOK_DEV)
    expert_ids_turns = jax.random.permutation(jax.random.fold_in(streams_of[1], 3), TOKENS // TOK_DEV)
    expert_ids = jax.vmap(lambda own, number: routed_block(jax.random.fold_in(streams_of[1], 2), own, number, TOK_DEV, EXPERTS, TOP, CAP, 2))(expert_ids_keys, expert_ids_turns).reshape((TOKENS, TOP))
    combine_weights = jnp.clip(0.1 + 0.9 * jax.random.uniform(streams_of[2], (TOKENS, TOP), jnp.float32) ** shard_levels(streams_of[2], (TOKENS, TOP), ((0, 128),), -0.2, 0.2), 0.1, 1.0)
    expert_gate = noise(streams_of[3], (EXPERTS, D, FF), D ** -0.5, 0.09375, ((0, 128),))
    expert_up = noise(streams_of[4], (EXPERTS, D, FF), D ** -0.5, 0.09375, ((0, 128),))
    expert_down = noise(streams_of[5], (EXPERTS, FF, D), FF ** -0.5, 0.1875, ((0, 128),))
    shared_gate = noise(streams_of[6], (D, SFF), D ** -0.5, 0.09375, ((1, 8),))
    shared_up = noise(streams_of[7], (D, SFF), D ** -0.5, 0.09375, ((1, 8),))
    shared_down = noise(streams_of[8], (SFF, D), SFF ** -0.5, 0.1875, ((0, 8),))
    return dict(tokens=tokens, expert_ids=expert_ids, combine_weights=combine_weights, expert_gate=expert_gate, expert_up=expert_up, expert_down=expert_down, shared_gate=shared_gate, shared_up=shared_up, shared_down=shared_down)


def expert_mlp(token_rows, gate_w, up_w, down_w):
    gate_proj = jnp.dot(token_rows, gate_w, preferred_element_type=jnp.float32)
    up_proj = jnp.dot(token_rows, up_w, preferred_element_type=jnp.float32)
    hidden = (jax.nn.silu(gate_proj) * up_proj).astype(jnp.bfloat16)
    return jnp.dot(hidden, down_w, preferred_element_type=jnp.float32).astype(jnp.bfloat16)


def place_slots(choices, experts, capacity):
    flat_ids = choices.reshape(-1).astype(jnp.int32)
    onehot = (flat_ids[:, None] == jnp.arange(experts, dtype=jnp.int32)[None, :]).astype(jnp.int32)
    running = jnp.cumsum(onehot, axis=0)
    slot_rank = jnp.sum(onehot * running, axis=1) - 1
    return flat_ids * capacity + slot_rank


def reference(tokens, expert_ids, combine_weights, expert_gate, expert_up, expert_down, shared_gate, shared_up, shared_down):
    devices = N_ROW * N_COL
    experts = devices
    per_device = expert_ids.reshape(devices, TOK_DEV, TOP)
    targets = jax.vmap(lambda chosen: place_slots(chosen, experts, CAP))(per_device)
    owner_row = jnp.arange(TOK_DEV * TOP, dtype=jnp.int32) // TOP

    def make_table(target):
        return jnp.full((experts * CAP,), -1, jnp.int32).at[target].set(owner_row)

    tables = jax.vmap(make_table)(targets)
    filled = tables >= 0
    global_rows = jnp.maximum(tables, 0) + (jnp.arange(devices, dtype=jnp.int32) * TOK_DEV)[:, None]

    def one_expert(inputs):
        number, gate_w, up_w, down_w = inputs
        row_index = lax.dynamic_slice_in_dim(global_rows, number * CAP, CAP, 1).reshape(-1)
        live = lax.dynamic_slice_in_dim(filled, number * CAP, CAP, 1).reshape(-1)
        token_rows = jnp.where(live[:, None], tokens[row_index], jnp.zeros((), jnp.bfloat16))
        return expert_mlp(token_rows, gate_w, up_w, down_w)

    results = lax.map(one_expert, (jnp.arange(experts, dtype=jnp.int32), expert_gate, expert_up, expert_down))
    flat_results = results.reshape(-1, D)

    def combine_device(inputs):
        source, target, weights = inputs
        expert_of = target // CAP
        slot_of = target % CAP
        index = expert_of * (devices * CAP) + source * CAP + slot_of
        picked = flat_results[index].reshape(TOK_DEV, TOP, D)
        return jnp.sum(picked.astype(jnp.float32) * weights[:, :, None], axis=1)

    routed = lax.map(combine_device, (jnp.arange(devices, dtype=jnp.int32), targets, combine_weights.reshape(devices, TOK_DEV, TOP)))
    routed = routed.reshape(TOKENS, D)
    gate_proj = jnp.dot(tokens, shared_gate, preferred_element_type=jnp.float32)
    up_proj = jnp.dot(tokens, shared_up, preferred_element_type=jnp.float32)
    shared_hidden = (jax.nn.silu(gate_proj) * up_proj).astype(jnp.bfloat16)
    shared = jnp.dot(shared_hidden, shared_down, preferred_element_type=jnp.float32)
    return (routed + shared).astype(jnp.bfloat16)
```

```python
import functools

import jax
import jax.numpy as jnp
from jax import lax
from jax.experimental import pallas as pl
from jax.experimental.pallas import tpu as pltpu
from jax.sharding import PartitionSpec as P

D = 3584
FF = 1024
T = 128
CAP = 5
DC = 512
NC = D // DC
PEERS = 16
SRC = 8
ROWS = CAP * SRC
ALL = PEERS * ROWS
LAG_B = 2
LAG_R = 2
LAG_F = 1
MESH = pl.DeviceIdType.MESH
bf16 = jnp.bfloat16
f32 = jnp.float32


def kernel(
    tok_hbm, meta_hbm, wg_hbm, wu_hbm, wd_hbm, sg_hbm, su_hbm, sd_hbm,
    out_ref,
    tok, snd, arr, ret, stage, acc, hid, pmat, cmat, wgu, wdn, wsh, wsd, sacc, shid,
    psend, prcv, ysend, yrcv, oacc, mt,
    ld, g_s, g_r, b_s, b_r, m_l, m_s, m_r, mb, a_s, a_r, r_s, r_r, w_s, w_l, wg_l, wd_l, p_s, p_r, y_s, y_r,
):
    row = lax.axis_index("row")
    col = lax.axis_index("col")
    y, x_lo = row // 2, row % 2
    z, x_hi, k = col // 4, (col // 2) % 2, col % 2
    x = x_hi * 2 + x_lo

    def dev(dx, dy, dz, dk):
        xx, yy, zz, kk = (x + dx) % 4, (y + dy) % 4, (z + dz) % 4, (k + dk) % 2
        return (yy * 2 + xx % 2, zz * 4 + (xx // 2) * 2 + kk)

    def remote(src, dst, ssem, rsem, where):
        return pltpu.make_async_remote_copy(
            src, dst, ssem, rsem, device_id=where, device_id_type=MESH
        )

    def wait_bytes(ref, sem):
        pltpu.make_async_copy(ref, ref, sem).wait()

    native = x_lo == k

    def tok_load(c):
        return pltpu.make_async_copy(
            tok_hbm.at[:, pl.ds(c * DC, DC)], tok.at[c, 0], ld.at[c]
        )

    meta_copy = pltpu.make_async_copy(meta_hbm, mt.at[0], m_l)
    meta_copy.start()
    for c in range(NC):
        tok_load(c).start()

    def wgu_load(c, slot):
        rows = pl.ds(c * DC, DC)
        return (
            pltpu.make_async_copy(wg_hbm.at[rows, :], wgu.at[slot, :, pl.ds(0, FF)], wg_l.at[slot, 0]),
            pltpu.make_async_copy(wu_hbm.at[rows, :], wgu.at[slot, :, pl.ds(FF, FF)], wg_l.at[slot, 1]),
        )

    def wdn_load(n, slot):
        return pltpu.make_async_copy(
            wd_hbm.at[:, pl.ds(n * DC, DC)], wdn.at[slot], wd_l.at[slot]
        )

    for slot in range(2):
        for copy in wgu_load(slot, slot):
            copy.start()
        wdn_load(slot, slot).start()

    barrier = pltpu.get_barrier_semaphore()
    plane = [(i // 4, 0, i % 4, 0) for i in range(1, PEERS)]
    friends = plane + [(0, 1, 0, 0), (0, 2, 0, 0), (0, 3, 0, 0), (0, 0, 0, 1)]
    for offset in friends:
        pl.semaphore_signal(barrier, inc=1, device_id=dev(*offset), device_id_type=MESH)
    pl.semaphore_wait(barrier, len(friends))

    meta_copy.wait()

    def meta_send(dy):
        return remote(mt.at[0], mt.at[4 - dy], m_s.at[dy], m_r.at[4 - dy], dev(0, dy, 0, 0))

    for dy in range(1, 4):
        meta_send(dy).start()

    def gather_send(c, dy):
        return remote(
            tok.at[c, 0], tok.at[c, 4 - dy], g_s.at[c, dy], g_r.at[c, 4 - dy], dev(0, dy, 0, 0)
        )

    def gather_start(c):
        tok_load(c).wait()
        for dy in range(1, 4):
            gather_send(c, dy).start()

    for c in range(2):
        gather_start(c)

    def shared_pieces():
        lanes = (pl.ds(0, 128), pl.ds(128, 128))
        return (
            (sg_hbm, wsh.at[:, :, lanes[0]], 1),
            (su_hbm, wsh.at[:, :, lanes[1]], 3),
            (sd_hbm.at[pl.ds(0, 64)], wsd.at[pl.ds(0, 64)], 1),
            (sd_hbm.at[pl.ds(64, 64)], wsd.at[pl.ds(64, 64)], 3),
        )

    @pl.when(native)
    def _():
        for i, (src, dst, dx) in enumerate(shared_pieces()):
            pltpu.make_async_copy(src, dst, w_l.at[i]).start()
            remote(src, dst, w_s.at[i], w_l.at[i], dev(dx, 0, 0, 0)).start()

    for dy in range(1, 4):
        meta_send(dy).wait_recv()
    meta_swap = remote(mt.at[pl.ds(0, 4)], mt.at[pl.ds(4, 4)], mb.at[0], mb.at[1], dev(0, 0, 0, 1))
    meta_swap.start()
    meta_swap.wait_recv()

    i16 = lax.broadcasted_iota(jnp.int32, (PEERS, T), 0)
    xe = (x + lax.shift_right_logical(i16, 2)) & 3
    ze = (z + (i16 & 3)) & 3
    expert = (y * 2 + (xe & 1)) * 16 + ze * 4 + lax.shift_right_logical(xe, 1) * 2 + k
    expert = expert.astype(f32)
    before = (
        lax.broadcasted_iota(jnp.int32, (T, T), 0) < lax.broadcasted_iota(jnp.int32, (T, T), 1)
    ).astype(f32).astype(bf16)
    q = lax.broadcasted_iota(jnp.int32, (ROWS, T), 0)
    q_src = q & 7
    q_slot = lax.shift_right_logical(q, 3).astype(f32)

    def build(s, carry):
        m = mt[s]
        named = jnp.zeros((PEERS, T), f32)
        weight = jnp.zeros((PEERS, T), f32)
        for j in range(4):
            hit = m[j : j + 1, :] == expert
            named = named + jnp.where(hit, 1.0, 0.0)
            weight = weight + jnp.where(hit, m[4 + j : 5 + j, :], 0.0)
        rank = jnp.dot(named.astype(bf16), before, preferred_element_type=f32)
        rank = jnp.where(named > 0.5, rank, -1.0)
        slot = jnp.where(q_src == s, q_slot, -9.0)
        here = rank[:, None, :] == slot[None, :, :]
        cols = pl.ds(pl.multiple_of(s * T, T), T)
        pmat[:, cols] = jnp.where(here, 1.0, 0.0).reshape(ALL, T).astype(bf16)
        scaled = jnp.where(here, weight[:, None, :], 0.0).reshape(ALL, T)
        cmat[cols, :] = scaled.T.astype(bf16)
        return carry

    lax.fori_loop(0, SRC, build, 0)

    acc[...] = jnp.zeros_like(acc)
    sacc[...] = jnp.zeros_like(sacc)

    def out_send(c, i):
        return remote(snd.at[c, i], arr.at[c, i], a_s.at[c], a_r.at[c], dev(i // 4, 0, i % 4, 0))

    def back_send(n, i):
        return remote(
            snd.at[n, i], ret.at[n, i], r_s.at[n], r_r.at[n], dev(4 - i // 4, 0, 4 - i % 4, 0)
        )

    def swap(c):
        return remote(
            tok.at[c, pl.ds(0, 4)], tok.at[c, pl.ds(4, 4)], b_s.at[c], b_r.at[c], dev(0, 0, 0, 1)
        )

    def rows_of(ref, c):
        return ref[c].astype(f32).reshape(ALL, DC).astype(bf16)

    def forward(it, carry):
        @pl.when(it < NC)
        def _():
            c = it
            for dy in range(1, 4):
                gather_send(c, dy).wait_recv()
            swap(c).start()

            @pl.when(c + 2 < NC)
            def _():
                gather_start(c + 2)

            swap(c).wait_recv()
            for h in range(DC // 256):
                cols = slice(h * 256, h * 256 + 256)
                rhs = tok[c, :, :, cols].reshape(SRC * T, 256)
                packed = jnp.dot(pmat[...], rhs, preferred_element_type=f32)
                packed = packed.reshape(PEERS, CAP, SRC, 256).astype(bf16)
                snd[c, :, :, :, cols] = packed
                arr[c, 0, :, :, cols] = packed[0]
            for i in range(1, PEERS):
                out_send(c, i).start()

        @pl.when(it >= LAG_B)
        def _():
            c = it - LAG_B
            slot = c % 2

            @pl.when(c == 0)
            def _():
                for i, (_, dst, _) in enumerate(shared_pieces()):
                    wait_bytes(dst, w_l.at[i])

            sacc[...] += jnp.dot(
                tok[c].reshape(SRC * T, DC), wsh[c], preferred_element_type=f32
            )
            wait_bytes(arr.at[c, pl.ds(1, PEERS - 1)], a_r.at[c])
            stage[...] = rows_of(arr, c)
            for copy in wgu_load(c, slot):
                copy.wait()
            for h in range(2 * FF // 256):
                cols = slice(h * 256, h * 256 + 256)
                acc[:, cols] += jnp.dot(stage[...], wgu[slot, :, cols], preferred_element_type=f32)

            @pl.when(c + 2 < NC)
            def _():
                for copy in wgu_load(c + 2, slot):
                    copy.start()

        return carry

    lax.fori_loop(0, NC + LAG_B, forward, 0)

    def silu_mul(gate, up):
        return (gate / (1.0 + jnp.exp(-gate)) * up).astype(bf16)

    for h in range(FF // 256):
        cols = slice(h * 256, h * 256 + 256)
        hid[:, cols] = silu_mul(acc[:, cols], acc[:, FF + h * 256 : FF + h * 256 + 256])
    shid[...] = silu_mul(sacc[:, 0:128], sacc[:, 128:256])

    def part_send(n):
        return remote(psend.at[n % 2], prcv.at[n], p_s.at[n], p_r.at[n], dev(0, 0, 0, 1))

    def line_send(n, dy):
        return remote(
            ysend.at[n % 2, dy - 1], yrcv.at[n, 3 - dy], y_s.at[n], y_r.at[n], dev(0, dy, 0, 0)
        )

    def backward(it, carry):
        @pl.when(it < NC)
        def _():
            n = it
            slot = n % 2
            wait_bytes(snd.at[n, pl.ds(1, PEERS - 1)], a_s.at[n])
            wdn_load(n, slot).wait()
            for h in range(DC // 256):
                cols = slice(h * 256, h * 256 + 256)
                done = jnp.dot(hid[...], wdn[slot, :, cols], preferred_element_type=f32)
                done = done.reshape(PEERS, CAP, SRC, 256).astype(bf16)
                snd[n, :, :, :, cols] = done
                ret[n, 0, :, :, cols] = done[0]
            for i in range(1, PEERS):
                back_send(n, i).start()

            @pl.when(n + 2 < NC)
            def _():
                wdn_load(n + 2, slot).start()

        @pl.when(jnp.logical_and(it >= LAG_R, it < NC + LAG_R))
        def _():
            n = it - LAG_R

            @pl.when(n >= 2)
            def _():
                part_send(n - 2).wait_send()
                wait_bytes(ysend.at[n % 2], y_s.at[n - 2])

            wait_bytes(ret.at[n, pl.ds(1, PEERS - 1)], r_r.at[n])
            stage[...] = rows_of(ret, n)
            cols = pl.ds(pl.multiple_of(n * DC, DC), DC)
            half = SRC * T // 2
            for lo in (half, 0):
                rows = pl.ds(lo, half)
                part = jnp.dot(cmat[rows, :], stage[...], preferred_element_type=f32)
                part = part + jnp.dot(shid[rows, :], wsd[:, cols], preferred_element_type=f32)
                if lo:
                    psend[n % 2] = part.astype(bf16)
                    part_send(n).start()
                else:
                    kept = part
            part_send(n).wait_recv()
            total = kept + prcv[n].astype(f32)
            for dy in range(1, 4):
                ysend[n % 2, dy - 1] = total[dy * T : dy * T + T].astype(bf16)
                line_send(n, dy).start()
            oacc[n] = total[0:T]

        @pl.when(it >= LAG_R + LAG_F)
        def _():
            n = it - LAG_R - LAG_F
            wait_bytes(yrcv.at[n], y_r.at[n])
            total = oacc[n]
            for j in range(3):
                total = total + yrcv[n, j].astype(f32)
            out_ref[:, pl.ds(pl.multiple_of(n * DC, DC), DC)] = total.astype(bf16)

        return carry

    lax.fori_loop(0, NC + LAG_R + LAG_F, backward, 0)

    for dy in range(1, 4):
        meta_send(dy).wait_send()
    meta_swap.wait_send()

    def drain(c, carry):
        for dy in range(1, 4):
            gather_send(c, dy).wait_send()
        swap(c).wait_send()
        wait_bytes(snd.at[c, pl.ds(1, PEERS - 1)], r_s.at[c])
        return carry

    lax.fori_loop(0, NC, drain, 0)
    for n in (NC - 2, NC - 1):
        part_send(n).wait_send()
        wait_bytes(ysend.at[n % 2], y_s.at[n])

    @pl.when(native)
    def _():
        for i, (src, dst, dx) in enumerate(shared_pieces()):
            remote(src, dst, w_s.at[i], w_l.at[i], dev(dx, 0, 0, 0)).wait_send()


def per_device(tokens, ids, weights, gate, up, down, sgate, sup, sdown):
    meta = jnp.concatenate([ids.T.astype(f32), weights.T], axis=0)
    dma = pltpu.SemaphoreType.DMA
    half = SRC * T // 2
    scratch = [
        pltpu.VMEM((NC, SRC, T, DC), bf16),
        pltpu.VMEM((NC, PEERS, CAP, SRC, DC), bf16),
        pltpu.VMEM((NC, PEERS, CAP, SRC, DC), bf16),
        pltpu.VMEM((NC, PEERS, CAP, SRC, DC), bf16),
        pltpu.VMEM((ALL, DC), bf16),
        pltpu.VMEM((ALL, 2 * FF), f32),
        pltpu.VMEM((ALL, FF), bf16),
        pltpu.VMEM((ALL, SRC * T), bf16),
        pltpu.VMEM((SRC * T, ALL), bf16),
        pltpu.VMEM((2, DC, 2 * FF), bf16),
        pltpu.VMEM((2, FF, DC), bf16),
        pltpu.VMEM((NC, DC, 256), bf16),
        pltpu.VMEM((128, D), bf16),
        pltpu.VMEM((SRC * T, 256), f32),
        pltpu.VMEM((SRC * T, 128), bf16),
        pltpu.VMEM((2, half, DC), bf16),
        pltpu.VMEM((NC, half, DC), bf16),
        pltpu.VMEM((2, 3, T, DC), bf16),
        pltpu.VMEM((NC, 3, T, DC), bf16),
        pltpu.VMEM((NC, T, DC), f32),
        pltpu.VMEM((SRC, 8, T), f32),
        dma((NC,)),
        dma((NC, 4)),
        dma((NC, 4)),
        dma((NC,)),
        dma((NC,)),
        dma,
        dma((4,)),
        dma((4,)),
        dma((2,)),
        dma((NC,)),
        dma((NC,)),
        dma((NC,)),
        dma((NC,)),
        dma((4,)),
        dma((4,)),
        dma((2, 2)),
        dma((2,)),
        dma((NC,)),
        dma((NC,)),
        dma((NC,)),
        dma((NC,)),
    ]
    hbm = pl.BlockSpec(memory_space=pl.ANY)
    return pl.pallas_call(
        kernel,
        out_shape=jax.ShapeDtypeStruct((T, D), bf16),
        in_specs=[hbm] * 8,
        out_specs=pl.BlockSpec(memory_space=pltpu.VMEM),
        scratch_shapes=scratch,
        cost_estimate=pl.CostEstimate(
            flops=2 * ALL * D * 3 * FF + 2 * SRC * T * D * 3 * 128,
            bytes_accessed=3 * D * FF * 2 + 4 * T * D,
            transcendentals=ALL * FF,
        ),
        compiler_params=pltpu.CompilerParams(
            collective_id=1, has_side_effects=True, vmem_limit_bytes=60 * 2**20
        ),
    )(
        tokens, meta, gate[0], up[0], down[0],
        sgate.reshape(NC, DC, 128), sup.reshape(NC, DC, 128), sdown,
    )


def solution(mesh):
    both = ("row", "col")
    placed = (
        P(both, None),
        P(both, None),
        P(both, None),
        P(both, None, None),
        P(both, None, None),
        P(both, None, None),
        P(None, "row"),
        P(None, "row"),
        P("row", None),
    )
    return jax.shard_map(
        per_device, mesh=mesh, in_specs=placed, out_specs=P(both, None), check_vma=False
    )
```

```python
import functools

import jax
import jax.numpy as jnp
from jax import lax
from jax.experimental import pallas as pl
from jax.experimental.pallas import tpu as pltpu
from jax.sharding import PartitionSpec as P

D = 3584
FF = 1024
T = 128
CAP = 5
DC = 256
NC = D // DC
PEERS = 16
SRC = 8
CUT = 3
RA = PEERS * CUT * SRC
ALL = PEERS * CAP * SRC
WHOLE_F = 8
SPLIT_R = 4
SLOTS_GU = NC - WHOLE_F
SLOTS_D = SPLIT_R
LAG_B = 3
LAG_R = 4
LAG_F = 3
LAG_S = 4
KEEP = 4
MESH = pl.DeviceIdType.MESH
bf16 = jnp.bfloat16
f32 = jnp.float32


def kernel(
    tok_hbm, ids_hbm, cw_hbm, wg_hbm, wu_hbm, wd_hbm, sg_hbm, su_hbm, sd_hbm,
    out_ref,
    tok, snd, arr, ret, stage, acc, hid, pmat, cmat, wgu, wdn, wsh, wsd, sacc, shid,
    psend, prcv, ysend, yrcv, oacc, mt, ids_v, cw_v,
    ld, g_s, g_r, b_s, b_r, m_l, m_s, m_r, a_s, a_r, a_b, r_s, r_r, r_b, w_s, w_l, wg_l, wd_l, p_s, p_r, y_s, y_r,
):
    row = lax.axis_index("row")
    col = lax.axis_index("col")
    y, x_lo = row // 2, row % 2
    z, x_hi, k = col // 4, (col // 2) % 2, col % 2
    x = x_hi * 2 + x_lo

    def dev(dx, dy, dz, dk):
        xx, yy, zz, kk = (x + dx) % 4, (y + dy) % 4, (z + dz) % 4, (k + dk) % 2
        return (yy * 2 + xx % 2, zz * 4 + (xx // 2) * 2 + kk)

    def remote(src, dst, ssem, rsem, where):
        return pltpu.make_async_remote_copy(
            src, dst, ssem, rsem, device_id=where, device_id_type=MESH
        )

    def wait_bytes(ref, sem):
        pltpu.make_async_copy(ref, ref, sem).wait()

    native = x_lo == k

    barrier = pltpu.get_barrier_semaphore()
    plane = [(i // 4, 0, i % 4, 0) for i in range(1, PEERS)]
    line = [(0, dy, 0, dk) for dk in range(2) for dy in range(4)][1:]
    for offset in plane + line:
        pl.semaphore_signal(barrier, inc=1, device_id=dev(*offset), device_id_type=MESH)

    def tok_load(c):
        return pltpu.make_async_copy(
            tok_hbm.at[:, pl.ds(c * DC, DC)], tok.at[c, 0], ld.at[c]
        )

    meta_copies = (
        pltpu.make_async_copy(ids_hbm, ids_v, m_l.at[0]),
        pltpu.make_async_copy(cw_hbm, cw_v, m_l.at[1]),
    )
    for copy in meta_copies:
        copy.start()
    for c in range(NC):
        tok_load(c).start()

    def wgu_load(c, slot):
        rows = pl.ds(c * DC, DC)
        return (
            pltpu.make_async_copy(wg_hbm.at[rows, :], wgu.at[slot, :, pl.ds(0, FF)], wg_l.at[slot, 0]),
            pltpu.make_async_copy(wu_hbm.at[rows, :], wgu.at[slot, :, pl.ds(FF, FF)], wg_l.at[slot, 1]),
        )

    def wdn_load(n, slot):
        return pltpu.make_async_copy(
            wd_hbm.at[:, pl.ds(n * DC, DC)], wdn.at[slot], wd_l.at[slot]
        )

    acc[...] = jnp.zeros_like(acc)
    sacc[...] = jnp.zeros_like(sacc)
    for copy in meta_copies:
        copy.wait()
    mt[0, 0:4, :] = ids_v[...].astype(f32)
    mt[0, 4:8, :] = cw_v[...]
    pl.semaphore_wait(barrier, len(plane + line))

    def meta_send(j):
        dk, dy = j // 4, j % 4
        there = dk * 4 + (4 - dy) % 4
        return remote(mt.at[0], mt.at[there], m_s.at[j], m_r.at[there], dev(0, dy, 0, dk))

    for j in range(1, SRC):
        meta_send(j).start()

    def gather_send(c, dy):
        return remote(
            tok.at[c, 0], tok.at[c, 4 - dy], g_s.at[c, dy], g_r.at[c, 4 - dy], dev(0, dy, 0, 0)
        )

    def gather_start(c):
        tok_load(c).wait()
        for dy in range(1, 4):
            gather_send(c, dy).start()

    gather_start(0)

    GATE, UP, DOWN = range(3)

    def quarter(w, q):
        if w == GATE:
            return sg_hbm.at[:, q], wsh.at[0, :, q]
        if w == UP:
            return su_hbm.at[:, q], wsh.at[1, :, q]
        return sd_hbm.at[q], wsd.at[q]

    def across_x(w):
        moves = ((0, 1), (1, 1), (2, 3), (3, 3))
        return [
            remote(*quarter(w, q), w_s.at[q, w], w_l.at[q, w], dev(dx, 0, 0, 0)) for q, dx in moves
        ]

    def own(w):
        return [pltpu.make_async_copy(*quarter(w, q), w_l.at[q, w]) for q in range(4)]

    def weight_wait(w, qs):
        for q in qs:
            wait_bytes(quarter(w, q)[1], w_l.at[q, w])

    def rest_wait(w):
        weight_wait(w, range(4))

    @pl.when(native)
    def _():
        for w in (UP, GATE):
            for copy in across_x(w):
                copy.start()

    gather_start(1)
    for slot in range(SLOTS_GU):
        for copy in wgu_load(slot, slot):
            copy.start()
    for slot in range(SLOTS_D):
        wdn_load(slot, slot).start()

    @pl.when(native)
    def _():
        for w in (UP, GATE, DOWN):
            for copy in own(w):
                copy.start()

    gather_start(2)
    for j in range(1, SRC):
        meta_send(j).wait_recv()

    i16 = lax.broadcasted_iota(jnp.int32, (PEERS, T), 0)
    xe = (x + lax.shift_right_logical(i16, 2)) & 3
    ze = (z + (i16 & 3)) & 3
    expert = (y * 2 + (xe & 1)) * 16 + ze * 4 + lax.shift_right_logical(xe, 1) * 2 + k
    expert = expert.astype(f32)
    before = (
        lax.broadcasted_iota(jnp.int32, (T, T), 0) < lax.broadcasted_iota(jnp.int32, (T, T), 1)
    ).astype(f32).astype(bf16)
    parts = ((0, CUT, 0, RA), (CUT, CAP, RA, ALL))

    def build(s, carry):
        m = mt[s]
        named = jnp.zeros((PEERS, T), f32)
        weight = jnp.zeros((PEERS, T), f32)
        for j in range(4):
            hit = m[j : j + 1, :] == expert
            named = named + jnp.where(hit, 1.0, 0.0)
            weight = weight + jnp.where(hit, m[4 + j : 5 + j, :], 0.0)
        rank = jnp.dot(named.astype(bf16), before, preferred_element_type=f32)
        rank = jnp.where(named > 0.5, rank, -1.0)
        cols = pl.ds(pl.multiple_of(s * T, T), T)
        for s0, s1, r0, r1 in parts:
            q = lax.broadcasted_iota(jnp.int32, ((s1 - s0) * SRC, T), 0)
            q_slot = lax.shift_right_logical(q, 3).astype(f32) + s0
            slot = jnp.where((q & 7) == s, q_slot, -9.0)
            here = rank[:, None, :] == slot[None, :, :]
            pmat[r0:r1, cols] = jnp.where(here, 1.0, 0.0).reshape(r1 - r0, T).astype(bf16)
            scaled = jnp.where(here, weight[:, None, :], 0.0).reshape(r1 - r0, T)
            cmat[cols, r0:r1] = scaled.T.astype(bf16)
        return carry

    lax.fori_loop(0, SRC, build, 0)

    def out_send(c, i, s0, s1, sem):
        slots = pl.ds(s0, s1 - s0)
        return remote(snd.at[c, i, slots], arr.at[c, i, slots], a_s.at[c], sem.at[c], dev(i // 4, 0, i % 4, 0))

    def back_send(n, i, s0, s1, sem):
        slots = pl.ds(s0, s1 - s0)
        return remote(snd.at[n, i, slots], ret.at[n, i, slots], r_s.at[n], sem.at[n], dev(4 - i // 4, 0, 4 - i % 4, 0))

    def swap(c):
        return remote(
            tok.at[c, pl.ds(0, 4)], tok.at[c, pl.ds(4, 4)], b_s.at[c], b_r.at[c], dev(0, 0, 0, 1)
        )

    def put(ref, c, values, which):
        for s0, s1, r0, r1 in which:
            base = which[0][2]
            ref[c, :, s0:s1] = values[r0 - base : r1 - base].reshape(PEERS, s1 - s0, SRC, DC).astype(bf16)

    def put_own(ref, c, values, which):
        for s0, s1, r0, r1 in which:
            base = r0 - which[0][2]
            ref[c, 0, s0:s1] = values[base : base + (s1 - s0) * SRC].reshape(s1 - s0, SRC, DC).astype(bf16)

    def take(ref, c, which):
        for s0, s1, r0, r1 in which:
            stage[r0:r1, :] = ref[c, :, s0:s1].astype(f32).reshape(r1 - r0, DC).astype(bf16)

    def line_wait(c):
        for dy in range(1, 4):
            gather_send(c, dy).wait_recv()
        swap(c).start()

    line_wait(0)
    gather_start(3)

    peers = pl.ds(1, PEERS - 1)

    def expert_dot(slot, r0, r1):
        for h in range(2 * FF // 256):
            cols = slice(h * 256, h * 256 + 256)
            acc[r0:r1, cols] += jnp.dot(stage[r0:r1, :], wgu[slot, :, cols], preferred_element_type=f32)

    def shared_dot(c):
        weights = jnp.concatenate([wsh[j, c].reshape(DC, 128) for j in range(2)], axis=1)
        sacc[...] += jnp.dot(tok[c].reshape(SRC * T, DC), weights, preferred_element_type=f32)

    def forward(it, carry):
        @pl.when(it < NC)
        def _():
            c = it
            swap(c).wait_recv()
            packed = jnp.dot(pmat[...], tok[c].reshape(SRC * T, DC), preferred_element_type=f32)
            put(snd, c, packed, parts)
            put_own(arr, c, packed, parts)

            @pl.when(c < WHOLE_F)
            def _():
                for i in range(1, PEERS):
                    out_send(c, i, 0, CAP, a_r).start()

            @pl.when(c >= WHOLE_F)
            def _():
                for i in range(1, PEERS):
                    out_send(c, i, 0, CUT, a_r).start()

            @pl.when(c == NC - 1)
            def _():
                def rest(cc, carry):
                    for i in range(1, PEERS):
                        out_send(cc, i, CUT, CAP, a_b).start()
                    return carry

                lax.fori_loop(WHOLE_F, NC, rest, 0)

            @pl.when(jnp.logical_and(c == 3, native))
            def _():
                for copy in across_x(DOWN):
                    copy.start()

            @pl.when(c + 1 < NC)
            def _():
                line_wait(c + 1)

            @pl.when(c + 4 < NC)
            def _():
                gather_start(c + 4)

        @pl.when(it >= LAG_B)
        def _():
            c = it - LAG_B
            slot = c % SLOTS_GU

            @pl.when(c == LAG_S)
            def _():
                rest_wait(UP)
                rest_wait(GATE)

            @pl.when(c >= LAG_S)
            def _():
                shared_dot(c - LAG_S)

            for copy in wgu_load(c, slot):
                copy.wait()

            @pl.when(c < WHOLE_F)
            def _():
                wait_bytes(arr.at[c, peers], a_r.at[c])
                take(arr, c, parts)
                expert_dot(slot, 0, ALL)

                @pl.when(c + SLOTS_GU < NC)
                def _():
                    for copy in wgu_load(c + SLOTS_GU, slot):
                        copy.start()

            @pl.when(c >= WHOLE_F)
            def _():
                wait_bytes(arr.at[c, peers, pl.ds(0, CUT)], a_r.at[c])
                take(arr, c, parts[:1])
                expert_dot(slot, 0, RA)

        return carry

    lax.fori_loop(0, NC + LAG_B, forward, 0)

    def silu_mul(gate, up):
        return (gate / (1.0 + jnp.exp(-gate)) * up).astype(bf16)

    def activate(r0, r1):
        for h in range(FF // 256):
            cols = slice(h * 256, h * 256 + 256)
            hid[r0:r1, cols] = silu_mul(acc[r0:r1, cols], acc[r0:r1, FF + h * 256 : FF + h * 256 + 256])

    def down(n, which, sem):
        slot = n % SLOTS_D
        done = jnp.dot(hid[which[0][2] : which[-1][3], :], wdn[slot], preferred_element_type=f32)
        put(snd, n, done, which)
        put_own(ret, n, done, which)
        for i in range(1, PEERS):
            back_send(n, i, which[0][0], which[-1][1], sem).start()

    activate(0, RA)

    def down_a(n, carry):
        wait_bytes(snd.at[n, peers], a_s.at[n])
        wdn_load(n, n).wait()
        down(n, parts[:1], r_r)
        return carry

    lax.fori_loop(0, SPLIT_R, down_a, 0)
    def shared_rest(c, carry):
        shared_dot(c)
        return carry

    lax.fori_loop(NC - LAG_S, NC, shared_rest, 0)
    shid[...] = silu_mul(sacc[:, 0:128], sacc[:, 128:256])

    def late(c, carry):
        wait_bytes(arr.at[c, peers, pl.ds(CUT, CAP - CUT)], a_b.at[c])
        take(arr, c, parts[1:])
        expert_dot(c % SLOTS_GU, RA, ALL)
        return carry

    lax.fori_loop(WHOLE_F, NC, late, 0)
    activate(RA, ALL)

    def down_b(n, carry):
        down(n, parts[1:], r_b)
        wdn_load(n + SLOTS_D, n).start()
        return carry

    lax.fori_loop(0, SPLIT_R, down_b, 0)

    def part_send(n):
        return remote(psend.at[n % 2], prcv.at[n], p_s.at[n], p_r.at[n], dev(0, 0, 0, 1))

    def line_send(n, dy):
        return remote(
            ysend.at[n % KEEP, dy - 1], yrcv.at[n, 3 - dy], y_s.at[n], y_r.at[n], dev(0, dy, 0, 0)
        )

    half = SRC * T // 2

    def backward(it, carry):
        @pl.when(it < NC)
        def _():
            n = it
            slot = n % SLOTS_D
            wait_bytes(snd.at[n, peers], a_s.at[n])
            wdn_load(n, slot).wait()
            down(n, parts, r_r)

            @pl.when(n + SLOTS_D < NC)
            def _():
                wdn_load(n + SLOTS_D, slot).start()

        @pl.when(jnp.logical_and(it >= LAG_R + 1, it < NC + LAG_R + 1))
        def _():
            n = it - LAG_R - 1

            @pl.when(n >= KEEP)
            def _():
                wait_bytes(ysend.at[n % KEEP], y_s.at[n - KEEP])

            part_send(n).wait_recv()
            for dy in range(1, 4):
                rows = slice(dy * T, dy * T + T)
                ysend[n % KEEP, dy - 1] = (oacc[n % KEEP, rows] + prcv[n, rows].astype(f32)).astype(bf16)
                line_send(n, dy).start()

        @pl.when(it >= LAG_R + 1 + LAG_F)
        def _():
            n = it - LAG_R - 1 - LAG_F
            wait_bytes(yrcv.at[n], y_r.at[n])
            total = oacc[n % KEEP, 0:T] + prcv[n, 0:T].astype(f32)
            for j in range(3):
                total = total + yrcv[n, j].astype(f32)
            out_ref[:, pl.ds(pl.multiple_of(n * DC, DC), DC)] = total.astype(bf16)

        @pl.when(jnp.logical_and(it >= LAG_R, it < NC + LAG_R))
        def _():
            n = it - LAG_R

            @pl.when(n >= 2)
            def _():
                part_send(n - 2).wait_send()

            @pl.when(n < SPLIT_R)
            def _():
                wait_bytes(ret.at[n, peers, pl.ds(0, CUT)], r_r.at[n])
                wait_bytes(ret.at[n, peers, pl.ds(CUT, CAP - CUT)], r_b.at[n])

            @pl.when(n >= SPLIT_R)
            def _():
                wait_bytes(ret.at[n, peers], r_r.at[n])

            take(ret, n, parts)

            @pl.when(n == 0)
            def _():
                rest_wait(DOWN)

            cols = pl.ds(pl.multiple_of(n * DC, DC), DC)
            for lo in (half, 0):
                rows = pl.ds(lo, half)
                part = jnp.dot(cmat[rows, :], stage[...], preferred_element_type=f32)
                part = part + jnp.dot(
                    shid[rows, :], wsd[:, :, cols].reshape(128, DC), preferred_element_type=f32
                )
                if lo:
                    psend[n % 2] = part.astype(bf16)
                    part_send(n).start()
                else:
                    oacc[n % KEEP] = part

        return carry

    lax.fori_loop(SPLIT_R, NC + LAG_R + 1 + LAG_F, backward, 0)

    for j in range(1, SRC):
        meta_send(j).wait_send()

    def drain(c, carry):
        for dy in range(1, 4):
            gather_send(c, dy).wait_send()
        swap(c).wait_send()
        wait_bytes(snd.at[c, peers], r_s.at[c])
        return carry

    lax.fori_loop(0, NC, drain, 0)
    for n in (NC - 2, NC - 1):
        part_send(n).wait_send()
    for n in range(NC - KEEP, NC):
        wait_bytes(ysend.at[n % KEEP], y_s.at[n])

    @pl.when(native)
    def _():
        for w in (UP, GATE, DOWN):
            for copy in across_x(w):
                copy.wait_send()


def per_device(tokens, ids, weights, gate, up, down, sgate, sup, sdown):
    dma = pltpu.SemaphoreType.DMA
    half = SRC * T // 2
    scratch = [
        pltpu.VMEM((NC, SRC, T, DC), bf16),
        pltpu.VMEM((NC, PEERS, CAP, SRC, DC), bf16),
        pltpu.VMEM((NC, PEERS, CAP, SRC, DC), bf16),
        pltpu.VMEM((NC, PEERS, CAP, SRC, DC), bf16),
        pltpu.VMEM((ALL, DC), bf16),
        pltpu.VMEM((ALL, 2 * FF), f32),
        pltpu.VMEM((ALL, FF), bf16),
        pltpu.VMEM((ALL, SRC * T), bf16),
        pltpu.VMEM((SRC * T, ALL), bf16),
        pltpu.VMEM((SLOTS_GU, DC, 2 * FF), bf16),
        pltpu.VMEM((SLOTS_D, FF, DC), bf16),
        pltpu.VMEM((2, NC, 4, DC // 4, 128), bf16),
        pltpu.VMEM((4, 32, D), bf16),
        pltpu.VMEM((SRC * T, 256), f32),
        pltpu.VMEM((SRC * T, 128), bf16),
        pltpu.VMEM((2, half, DC), bf16),
        pltpu.VMEM((NC, half, DC), bf16),
        pltpu.VMEM((KEEP, 3, T, DC), bf16),
        pltpu.VMEM((NC, 3, T, DC), bf16),
        pltpu.VMEM((KEEP, half, DC), f32),
        pltpu.VMEM((SRC, 8, T), f32),
        pltpu.VMEM((4, T), jnp.int32),
        pltpu.VMEM((4, T), f32),
        dma((NC,)),
        dma((NC, 4)),
        dma((NC, 4)),
        dma((NC,)),
        dma((NC,)),
        dma((2,)),
        dma((SRC,)),
        dma((SRC,)),
        dma((NC,)),
        dma((NC,)),
        dma((NC,)),
        dma((NC,)),
        dma((NC,)),
        dma((NC,)),
        dma((4, 3)),
        dma((4, 3)),
        dma((SLOTS_GU, 2)),
        dma((SLOTS_D,)),
        dma((NC,)),
        dma((NC,)),
        dma((NC,)),
        dma((NC,)),
    ]
    hbm = pl.BlockSpec(memory_space=pl.ANY)
    return pl.pallas_call(
        kernel,
        out_shape=jax.ShapeDtypeStruct((T, D), bf16),
        in_specs=[hbm] * 9,
        out_specs=pl.BlockSpec(memory_space=pltpu.VMEM),
        scratch_shapes=scratch,
        cost_estimate=pl.CostEstimate(
            flops=2 * ALL * D * 3 * FF + 2 * SRC * T * D * 3 * 128,
            bytes_accessed=3 * D * FF * 2 + 4 * T * D,
            transcendentals=ALL * FF,
        ),
        compiler_params=pltpu.CompilerParams(
            collective_id=1, has_side_effects=True, vmem_limit_bytes=60 * 2**20
        ),
    )(
        tokens, ids.T, weights.T, gate[0], up[0], down[0],
        sgate.reshape(NC, 4, DC // 4, 128), sup.reshape(NC, 4, DC // 4, 128), sdown.reshape(4, 32, D),
    )


def solution(mesh):
    both = ("row", "col")
    placed = (
        P(both, None),
        P(both, None),
        P(both, None),
        P(both, None, None),
        P(both, None, None),
        P(both, None, None),
        P(None, "row"),
        P(None, "row"),
        P("row", None),
    )
    return jax.shard_map(
        per_device, mesh=mesh, in_specs=placed, out_specs=P(both, None), check_vma=False
    )
```

```python
import functools

import jax
import jax.numpy as jnp
from jax import lax
from jax.experimental import pallas as pl
from jax.experimental.pallas import tpu as pltpu
from jax.sharding import PartitionSpec as P

D = 3584
FF = 1024
T = 128
CAP = 5
DC = 256
NC = D // DC
PEERS = 16
SRC = 8
CUT = 3
RA = PEERS * CUT * SRC
ALL = PEERS * CAP * SRC
WHOLE_F = 13
SPLIT_R = 1
SLOTS_GU = 6
SLOTS_D = 4
LAG_B = 3
LAG_R = 4
LAG_F = 3
LAG_S = 4
KEEP = 4
MESH = pl.DeviceIdType.MESH
bf16 = jnp.bfloat16
f32 = jnp.float32


def kernel(
    tok_hbm, ids_hbm, cw_hbm, wg_hbm, wu_hbm, wd_hbm, sg_hbm, su_hbm, sd_hbm,
    out_ref,
    tok, snd, arr, ret, stage, acc, hid, pmat, cmat, wgu, wdn, wsh, wsd, sacc, shid,
    psend, prcv, ysend, yrcv, oacc, mt, ids_v, cw_v,
    ld, g_s, g_r, b_s, b_r, m_l, m_s, m_r, a_s, a_r, a_b, r_s, r_r, r_b, w_s, w_l, wg_l, wd_l, p_s, p_r, y_s, y_r,
):
    row = lax.axis_index("row")
    col = lax.axis_index("col")
    y, x_lo = row // 2, row % 2
    z, x_hi, k = col // 4, (col // 2) % 2, col % 2
    x = x_hi * 2 + x_lo

    def dev(dx, dy, dz, dk):
        xx, yy, zz, kk = (x + dx) % 4, (y + dy) % 4, (z + dz) % 4, (k + dk) % 2
        return (yy * 2 + xx % 2, zz * 4 + (xx // 2) * 2 + kk)

    def remote(src, dst, ssem, rsem, where):
        return pltpu.make_async_remote_copy(
            src, dst, ssem, rsem, device_id=where, device_id_type=MESH
        )

    def wait_bytes(ref, sem):
        pltpu.make_async_copy(ref, ref, sem).wait()

    native = x_lo == k

    barrier = pltpu.get_barrier_semaphore()
    plane = [(i // 4, 0, i % 4, 0) for i in range(1, PEERS)]
    line = [(0, dy, 0, dk) for dk in range(2) for dy in range(4)][1:]
    for offset in plane + line:
        pl.semaphore_signal(barrier, inc=1, device_id=dev(*offset), device_id_type=MESH)

    def tok_load(c):
        return pltpu.make_async_copy(
            tok_hbm.at[:, pl.ds(c * DC, DC)], tok.at[c, 0], ld.at[c]
        )

    meta_copies = (
        pltpu.make_async_copy(ids_hbm, ids_v, m_l.at[0]),
        pltpu.make_async_copy(cw_hbm, cw_v, m_l.at[1]),
    )
    for copy in meta_copies:
        copy.start()
    for c in range(NC):
        tok_load(c).start()

    def wgu_load(c, slot):
        rows = pl.ds(c * DC, DC)
        return (
            pltpu.make_async_copy(wg_hbm.at[rows, :], wgu.at[slot, :, pl.ds(0, FF)], wg_l.at[slot, 0]),
            pltpu.make_async_copy(wu_hbm.at[rows, :], wgu.at[slot, :, pl.ds(FF, FF)], wg_l.at[slot, 1]),
        )

    def wdn_load(n, slot):
        return pltpu.make_async_copy(
            wd_hbm.at[:, pl.ds(n * DC, DC)], wdn.at[slot], wd_l.at[slot]
        )

    acc[...] = jnp.zeros_like(acc)
    sacc[...] = jnp.zeros_like(sacc)
    for copy in meta_copies:
        copy.wait()
    mt[0, 0:4, :] = ids_v[...].astype(f32)
    mt[0, 4:8, :] = cw_v[...]
    pl.semaphore_wait(barrier, len(plane + line))

    def meta_send(j):
        dk, dy = j // 4, j % 4
        there = dk * 4 + (4 - dy) % 4
        return remote(mt.at[0], mt.at[there], m_s.at[j], m_r.at[there], dev(0, dy, 0, dk))

    for j in range(1, SRC):
        meta_send(j).start()

    def gather_send(c, dy):
        return remote(
            tok.at[c, 0], tok.at[c, 4 - dy], g_s.at[c, dy], g_r.at[c, 4 - dy], dev(0, dy, 0, 0)
        )

    def gather_start(c):
        tok_load(c).wait()
        for dy in range(1, 4):
            gather_send(c, dy).start()

    gather_start(0)

    GATE, UP, DOWN = range(3)

    def quarter(w, q):
        if w == GATE:
            return sg_hbm.at[:, q], wsh.at[0, :, q]
        if w == UP:
            return su_hbm.at[:, q], wsh.at[1, :, q]
        return sd_hbm.at[q], wsd.at[q]

    def across_x(w):
        moves = ((0, 1), (1, 1), (2, 3), (3, 3))
        return [
            remote(*quarter(w, q), w_s.at[q, w], w_l.at[q, w], dev(dx, 0, 0, 0)) for q, dx in moves
        ]

    def own(w):
        return [pltpu.make_async_copy(*quarter(w, q), w_l.at[q, w]) for q in range(4)]

    def weight_wait(w, qs):
        for q in qs:
            wait_bytes(quarter(w, q)[1], w_l.at[q, w])

    def rest_wait(w):
        weight_wait(w, range(4))

    @pl.when(native)
    def _():
        for w in (UP, GATE):
            for copy in across_x(w):
                copy.start()

    gather_start(1)
    for slot in range(SLOTS_GU):
        for copy in wgu_load(slot, slot):
            copy.start()
    for slot in range(SLOTS_D):
        wdn_load(slot, slot).start()

    @pl.when(native)
    def _():
        for w in (UP, GATE, DOWN):
            for copy in own(w):
                copy.start()

    gather_start(2)
    for j in range(1, SRC):
        meta_send(j).wait_recv()

    i16 = lax.broadcasted_iota(jnp.int32, (PEERS, T), 0)
    xe = (x + lax.shift_right_logical(i16, 2)) & 3
    ze = (z + (i16 & 3)) & 3
    expert = (y * 2 + (xe & 1)) * 16 + ze * 4 + lax.shift_right_logical(xe, 1) * 2 + k
    expert = expert.astype(f32)
    before = (
        lax.broadcasted_iota(jnp.int32, (T, T), 0) < lax.broadcasted_iota(jnp.int32, (T, T), 1)
    ).astype(f32).astype(bf16)
    parts = ((0, CUT, 0, RA), (CUT, CAP, RA, ALL))

    def build(s, carry):
        m = mt[s]
        named = jnp.zeros((PEERS, T), f32)
        weight = jnp.zeros((PEERS, T), f32)
        for j in range(4):
            hit = m[j : j + 1, :] == expert
            named = named + jnp.where(hit, 1.0, 0.0)
            weight = weight + jnp.where(hit, m[4 + j : 5 + j, :], 0.0)
        rank = jnp.dot(named.astype(bf16), before, preferred_element_type=f32)
        rank = jnp.where(named > 0.5, rank, -1.0)
        cols = pl.ds(pl.multiple_of(s * T, T), T)
        for s0, s1, r0, r1 in parts:
            q = lax.broadcasted_iota(jnp.int32, ((s1 - s0) * SRC, T), 0)
            q_slot = lax.shift_right_logical(q, 3).astype(f32) + s0
            slot = jnp.where((q & 7) == s, q_slot, -9.0)
            here = rank[:, None, :] == slot[None, :, :]
            pmat[r0:r1, cols] = jnp.where(here, 1.0, 0.0).reshape(r1 - r0, T).astype(bf16)
            scaled = jnp.where(here, weight[:, None, :], 0.0).reshape(r1 - r0, T)
            cmat[cols, r0:r1] = scaled.T.astype(bf16)
        return carry

    lax.fori_loop(0, SRC, build, 0)

    def out_send(c, i, s0, s1, sem):
        slots = pl.ds(s0, s1 - s0)
        return remote(snd.at[c, i, slots], arr.at[c, i, slots], a_s.at[c], sem.at[c], dev(i // 4, 0, i % 4, 0))

    def back_send(n, i, s0, s1, sem):
        slots = pl.ds(s0, s1 - s0)
        return remote(snd.at[n, i, slots], ret.at[n, i, slots], r_s.at[n], sem.at[n], dev(4 - i // 4, 0, 4 - i % 4, 0))

    def swap(c):
        return remote(
            tok.at[c, pl.ds(0, 4)], tok.at[c, pl.ds(4, 4)], b_s.at[c], b_r.at[c], dev(0, 0, 0, 1)
        )

    def put(ref, c, values, which):
        for s0, s1, r0, r1 in which:
            base = which[0][2]
            ref[c, :, s0:s1] = values[r0 - base : r1 - base].reshape(PEERS, s1 - s0, SRC, DC).astype(bf16)

    def put_own(ref, c, values, which):
        for s0, s1, r0, r1 in which:
            base = r0 - which[0][2]
            ref[c, 0, s0:s1] = values[base : base + (s1 - s0) * SRC].reshape(s1 - s0, SRC, DC).astype(bf16)

    def take(ref, c, which):
        for s0, s1, r0, r1 in which:
            stage[r0:r1, :] = ref[c, :, s0:s1].astype(f32).reshape(r1 - r0, DC).astype(bf16)

    def line_wait(c):
        for dy in range(1, 4):
            gather_send(c, dy).wait_recv()
        swap(c).start()

    line_wait(0)
    gather_start(3)

    peers = pl.ds(1, PEERS - 1)

    def expert_dot(slot, r0, r1):
        for h in range(2 * FF // 256):
            cols = slice(h * 256, h * 256 + 256)
            acc[r0:r1, cols] += jnp.dot(stage[r0:r1, :], wgu[slot, :, cols], preferred_element_type=f32)

    def shared_dot(c):
        weights = jnp.concatenate([wsh[j, c].reshape(DC, 128) for j in range(2)], axis=1)
        sacc[...] += jnp.dot(tok[c].reshape(SRC * T, DC), weights, preferred_element_type=f32)

    def forward(it, carry):
        @pl.when(it < NC)
        def _():
            c = it
            swap(c).wait_recv()
            packed = jnp.dot(pmat[...], tok[c].reshape(SRC * T, DC), preferred_element_type=f32)
            put(snd, c, packed, parts)
            put_own(arr, c, packed, parts)

            @pl.when(c < WHOLE_F)
            def _():
                for i in range(1, PEERS):
                    out_send(c, i, 0, CAP, a_r).start()

            @pl.when(c >= WHOLE_F)
            def _():
                for i in range(1, PEERS):
                    out_send(c, i, 0, CUT, a_r).start()

            @pl.when(c == NC - 1)
            def _():
                def rest(cc, carry):
                    for i in range(1, PEERS):
                        out_send(cc, i, CUT, CAP, a_b).start()
                    return carry

                lax.fori_loop(WHOLE_F, NC, rest, 0)

                @pl.when(native)
                def _():
                    for copy in across_x(DOWN):
                        copy.start()

            @pl.when(c + 1 < NC)
            def _():
                line_wait(c + 1)

            @pl.when(c + 4 < NC)
            def _():
                gather_start(c + 4)

        @pl.when(it >= LAG_B)
        def _():
            c = it - LAG_B
            slot = c % SLOTS_GU

            @pl.when(c == LAG_S)
            def _():
                rest_wait(UP)
                rest_wait(GATE)

            @pl.when(c >= LAG_S)
            def _():
                shared_dot(c - LAG_S)

            for copy in wgu_load(c, slot):
                copy.wait()

            @pl.when(c < WHOLE_F)
            def _():
                wait_bytes(arr.at[c, peers], a_r.at[c])
                take(arr, c, parts)
                expert_dot(slot, 0, ALL)

                @pl.when(c + SLOTS_GU < NC)
                def _():
                    for copy in wgu_load(c + SLOTS_GU, slot):
                        copy.start()

            @pl.when(c >= WHOLE_F)
            def _():
                wait_bytes(arr.at[c, peers, pl.ds(0, CUT)], a_r.at[c])
                take(arr, c, parts[:1])
                expert_dot(slot, 0, RA)

        return carry

    lax.fori_loop(0, NC + LAG_B, forward, 0)

    def silu_mul(gate, up):
        return (gate / (1.0 + jnp.exp(-gate)) * up).astype(bf16)

    def activate(r0, r1):
        for h in range(FF // 256):
            cols = slice(h * 256, h * 256 + 256)
            hid[r0:r1, cols] = silu_mul(acc[r0:r1, cols], acc[r0:r1, FF + h * 256 : FF + h * 256 + 256])

    def down(n, which, sem):
        slot = n % SLOTS_D
        done = jnp.dot(hid[which[0][2] : which[-1][3], :], wdn[slot], preferred_element_type=f32)
        put(snd, n, done, which)
        put_own(ret, n, done, which)
        for i in range(1, PEERS):
            back_send(n, i, which[0][0], which[-1][1], sem).start()

    activate(0, RA)

    def down_a(n, carry):
        wait_bytes(snd.at[n, peers], a_s.at[n])
        wdn_load(n, n).wait()
        down(n, parts[:1], r_r)
        return carry

    lax.fori_loop(0, SPLIT_R, down_a, 0)
    def shared_rest(c, carry):
        shared_dot(c)
        return carry

    lax.fori_loop(NC - LAG_S, NC, shared_rest, 0)
    shid[...] = silu_mul(sacc[:, 0:128], sacc[:, 128:256])

    def late(c, carry):
        wait_bytes(arr.at[c, peers, pl.ds(CUT, CAP - CUT)], a_b.at[c])
        take(arr, c, parts[1:])
        expert_dot(c % SLOTS_GU, RA, ALL)
        return carry

    lax.fori_loop(WHOLE_F, NC, late, 0)
    activate(RA, ALL)

    def down_b(n, carry):
        down(n, parts[1:], r_b)
        wdn_load(n + SLOTS_D, n).start()
        return carry

    lax.fori_loop(0, SPLIT_R, down_b, 0)

    def part_send(n):
        return remote(psend.at[n % 2], prcv.at[n], p_s.at[n], p_r.at[n], dev(0, 0, 0, 1))

    def line_send(n, dy):
        return remote(
            ysend.at[n % KEEP, dy - 1], yrcv.at[n, 3 - dy], y_s.at[n], y_r.at[n], dev(0, dy, 0, 0)
        )

    half = SRC * T // 2

    def backward(it, carry):
        @pl.when(it < NC)
        def _():
            n = it
            slot = n % SLOTS_D
            wait_bytes(snd.at[n, peers], a_s.at[n])
            wdn_load(n, slot).wait()
            down(n, parts, r_r)

            @pl.when(n + SLOTS_D < NC)
            def _():
                wdn_load(n + SLOTS_D, slot).start()

        @pl.when(jnp.logical_and(it >= LAG_R + 1, it < NC + LAG_R + 1))
        def _():
            n = it - LAG_R - 1

            @pl.when(n >= KEEP)
            def _():
                wait_bytes(ysend.at[n % KEEP], y_s.at[n - KEEP])

            part_send(n).wait_recv()
            for dy in range(1, 4):
                rows = slice(dy * T, dy * T + T)
                ysend[n % KEEP, dy - 1] = (oacc[n % KEEP, rows] + prcv[n, rows].astype(f32)).astype(bf16)
                line_send(n, dy).start()

        @pl.when(it >= LAG_R + 1 + LAG_F)
        def _():
            n = it - LAG_R - 1 - LAG_F
            wait_bytes(yrcv.at[n], y_r.at[n])
            total = oacc[n % KEEP, 0:T] + prcv[n, 0:T].astype(f32)
            for j in range(3):
                total = total + yrcv[n, j].astype(f32)
            out_ref[:, pl.ds(pl.multiple_of(n * DC, DC), DC)] = total.astype(bf16)

        @pl.when(jnp.logical_and(it >= LAG_R, it < NC + LAG_R))
        def _():
            n = it - LAG_R

            @pl.when(n >= 2)
            def _():
                part_send(n - 2).wait_send()

            @pl.when(n < SPLIT_R)
            def _():
                wait_bytes(ret.at[n, peers, pl.ds(0, CUT)], r_r.at[n])
                wait_bytes(ret.at[n, peers, pl.ds(CUT, CAP - CUT)], r_b.at[n])

            @pl.when(n >= SPLIT_R)
            def _():
                wait_bytes(ret.at[n, peers], r_r.at[n])

            take(ret, n, parts)

            @pl.when(n == 0)
            def _():
                rest_wait(DOWN)

            cols = pl.ds(pl.multiple_of(n * DC, DC), DC)
            for lo in (half, 0):
                rows = pl.ds(lo, half)
                part = jnp.dot(cmat[rows, :], stage[...], preferred_element_type=f32)
                part = part + jnp.dot(
                    shid[rows, :], wsd[:, :, cols].reshape(128, DC), preferred_element_type=f32
                )
                if lo:
                    psend[n % 2] = part.astype(bf16)
                    part_send(n).start()
                else:
                    oacc[n % KEEP] = part

        return carry

    lax.fori_loop(SPLIT_R, NC + LAG_R + 1 + LAG_F, backward, 0)

    for j in range(1, SRC):
        meta_send(j).wait_send()

    def drain(c, carry):
        for dy in range(1, 4):
            gather_send(c, dy).wait_send()
        swap(c).wait_send()
        wait_bytes(snd.at[c, peers], r_s.at[c])
        return carry

    lax.fori_loop(0, NC, drain, 0)
    for n in (NC - 2, NC - 1):
        part_send(n).wait_send()
    for n in range(NC - KEEP, NC):
        wait_bytes(ysend.at[n % KEEP], y_s.at[n])

    @pl.when(native)
    def _():
        for w in (UP, GATE, DOWN):
            for copy in across_x(w):
                copy.wait_send()


def per_device(tokens, ids, weights, gate, up, down, sgate, sup, sdown):
    dma = pltpu.SemaphoreType.DMA
    half = SRC * T // 2
    scratch = [
        pltpu.VMEM((NC, SRC, T, DC), bf16),
        pltpu.VMEM((NC, PEERS, CAP, SRC, DC), bf16),
        pltpu.VMEM((NC, PEERS, CAP, SRC, DC), bf16),
        pltpu.VMEM((NC, PEERS, CAP, SRC, DC), bf16),
        pltpu.VMEM((ALL, DC), bf16),
        pltpu.VMEM((ALL, 2 * FF), f32),
        pltpu.VMEM((ALL, FF), bf16),
        pltpu.VMEM((ALL, SRC * T), bf16),
        pltpu.VMEM((SRC * T, ALL), bf16),
        pltpu.VMEM((SLOTS_GU, DC, 2 * FF), bf16),
        pltpu.VMEM((SLOTS_D, FF, DC), bf16),
        pltpu.VMEM((2, NC, 4, DC // 4, 128), bf16),
        pltpu.VMEM((4, 32, D), bf16),
        pltpu.VMEM((SRC * T, 256), f32),
        pltpu.VMEM((SRC * T, 128), bf16),
        pltpu.VMEM((2, half, DC), bf16),
        pltpu.VMEM((NC, half, DC), bf16),
        pltpu.VMEM((KEEP, 3, T, DC), bf16),
        pltpu.VMEM((NC, 3, T, DC), bf16),
        pltpu.VMEM((KEEP, half, DC), f32),
        pltpu.VMEM((SRC, 8, T), f32),
        pltpu.VMEM((4, T), jnp.int32),
        pltpu.VMEM((4, T), f32),
        dma((NC,)),
        dma((NC, 4)),
        dma((NC, 4)),
        dma((NC,)),
        dma((NC,)),
        dma((2,)),
        dma((SRC,)),
        dma((SRC,)),
        dma((NC,)),
        dma((NC,)),
        dma((NC,)),
        dma((NC,)),
        dma((NC,)),
        dma((NC,)),
        dma((4, 3)),
        dma((4, 3)),
        dma((SLOTS_GU, 2)),
        dma((SLOTS_D,)),
        dma((NC,)),
        dma((NC,)),
        dma((NC,)),
        dma((NC,)),
    ]
    hbm = pl.BlockSpec(memory_space=pl.ANY)
    return pl.pallas_call(
        kernel,
        out_shape=jax.ShapeDtypeStruct((T, D), bf16),
        in_specs=[hbm] * 9,
        out_specs=pl.BlockSpec(memory_space=pltpu.VMEM),
        scratch_shapes=scratch,
        cost_estimate=pl.CostEstimate(
            flops=2 * ALL * D * 3 * FF + 2 * SRC * T * D * 3 * 128,
            bytes_accessed=3 * D * FF * 2 + 4 * T * D,
            transcendentals=ALL * FF,
        ),
        compiler_params=pltpu.CompilerParams(
            collective_id=1, has_side_effects=True, vmem_limit_bytes=60 * 2**20
        ),
    )(
        tokens, ids.T, weights.T, gate[0], up[0], down[0],
        sgate.reshape(NC, 4, DC // 4, 128), sup.reshape(NC, 4, DC // 4, 128), sdown.reshape(4, 32, D),
    )


def solution(mesh):
    both = ("row", "col")
    placed = (
        P(both, None),
        P(both, None),
        P(both, None),
        P(both, None, None),
        P(both, None, None),
        P(both, None, None),
        P(None, "row"),
        P(None, "row"),
        P("row", None),
    )
    return jax.shard_map(
        per_device, mesh=mesh, in_specs=placed, out_specs=P(both, None), check_vma=False
    )
```

```python
import functools

import jax
import jax.numpy as jnp
from jax import lax
from jax.experimental import pallas as pl
from jax.experimental.pallas import tpu as pltpu
from jax.sharding import PartitionSpec as P

D = 3584
FF = 1024
T = 128
CAP = 5
DC = 256
NC = D // DC
PEERS = 16
SRC = 8
CUT = 3
RA = PEERS * CUT * SRC
ALL = PEERS * CAP * SRC
WHOLE_F = 13
SPLIT_R = 1
SLOTS_GU = 6
SLOTS_D = 4
LAG_B = 3
LAG_R = 4
LAG_F = 3
LAG_S = 4
KEEP = 4
ORDER = sorted(range(1, PEERS), key=lambda i: -(min(i // 4, 4 - i // 4) + min(i % 4, 4 - i % 4)))
MESH = pl.DeviceIdType.MESH
bf16 = jnp.bfloat16
f32 = jnp.float32


def kernel(
    tok_hbm, ids_hbm, cw_hbm, wg_hbm, wu_hbm, wd_hbm, sg_hbm, su_hbm, sd_hbm,
    out_ref,
    tok, snd, arr, ret, stage, acc, hid, pmat, cmat, wgu, wdn, wsh, wsd, sacc, shid,
    psend, prcv, ysend, yrcv, oacc, mt, ids_v, cw_v,
    ld, g_s, g_r, b_s, b_r, m_l, m_s, m_r, a_s, a_r, a_b, r_s, r_r, r_b, w_s, w_l, wg_l, wd_l, p_s, p_r, y_s, y_r,
):
    row = lax.axis_index("row")
    col = lax.axis_index("col")
    y, x_lo = row // 2, row % 2
    z, x_hi, k = col // 4, (col // 2) % 2, col % 2
    x = x_hi * 2 + x_lo

    def dev(dx, dy, dz, dk):
        xx, yy, zz, kk = (x + dx) % 4, (y + dy) % 4, (z + dz) % 4, (k + dk) % 2
        return (yy * 2 + xx % 2, zz * 4 + (xx // 2) * 2 + kk)

    def remote(src, dst, ssem, rsem, where):
        return pltpu.make_async_remote_copy(
            src, dst, ssem, rsem, device_id=where, device_id_type=MESH
        )

    def wait_bytes(ref, sem):
        pltpu.make_async_copy(ref, ref, sem).wait()

    native = x_lo == k

    barrier = pltpu.get_barrier_semaphore()
    plane = [(i // 4, 0, i % 4, 0) for i in range(1, PEERS)]
    line = [(0, dy, 0, dk) for dk in range(2) for dy in range(4)][1:]
    for offset in plane + line:
        pl.semaphore_signal(barrier, inc=1, device_id=dev(*offset), device_id_type=MESH)

    def tok_load(c):
        return pltpu.make_async_copy(
            tok_hbm.at[:, pl.ds(c * DC, DC)], tok.at[c, 0], ld.at[c]
        )

    meta_copies = (
        pltpu.make_async_copy(ids_hbm, ids_v, m_l.at[0]),
        pltpu.make_async_copy(cw_hbm, cw_v, m_l.at[1]),
    )
    for copy in meta_copies:
        copy.start()
    for c in range(NC):
        tok_load(c).start()

    def wgu_load(c, slot):
        rows = pl.ds(c * DC, DC)
        return (
            pltpu.make_async_copy(wg_hbm.at[rows, :], wgu.at[slot, :, pl.ds(0, FF)], wg_l.at[slot, 0]),
            pltpu.make_async_copy(wu_hbm.at[rows, :], wgu.at[slot, :, pl.ds(FF, FF)], wg_l.at[slot, 1]),
        )

    def wdn_load(n, slot):
        return pltpu.make_async_copy(
            wd_hbm.at[:, pl.ds(n * DC, DC)], wdn.at[slot], wd_l.at[slot]
        )

    acc[...] = jnp.zeros_like(acc)
    sacc[...] = jnp.zeros_like(sacc)
    for copy in meta_copies:
        copy.wait()
    mt[0, 0:4, :] = ids_v[...].astype(f32)
    mt[0, 4:8, :] = cw_v[...]
    pl.semaphore_wait(barrier, len(plane + line))

    def meta_send(j):
        dk, dy = j // 4, j % 4
        there = dk * 4 + (4 - dy) % 4
        return remote(mt.at[0], mt.at[there], m_s.at[j], m_r.at[there], dev(0, dy, 0, dk))

    for j in range(1, SRC):
        meta_send(j).start()

    def gather_send(c, dy):
        return remote(
            tok.at[c, 0], tok.at[c, 4 - dy], g_s.at[c, dy], g_r.at[c, 4 - dy], dev(0, dy, 0, 0)
        )

    def gather_start(c):
        tok_load(c).wait()
        for dy in range(1, 4):
            gather_send(c, dy).start()

    gather_start(0)

    GATE, UP, DOWN = range(3)

    def quarter(w, q):
        if w == GATE:
            return sg_hbm.at[:, q], wsh.at[0, :, q]
        if w == UP:
            return su_hbm.at[:, q], wsh.at[1, :, q]
        return sd_hbm.at[q], wsd.at[q]

    def across_x(w):
        moves = ((0, 1), (1, 1), (2, 3), (3, 3))
        return [
            remote(*quarter(w, q), w_s.at[q, w], w_l.at[q, w], dev(dx, 0, 0, 0)) for q, dx in moves
        ]

    def own(w):
        return [pltpu.make_async_copy(*quarter(w, q), w_l.at[q, w]) for q in range(4)]

    def weight_wait(w, qs):
        for q in qs:
            wait_bytes(quarter(w, q)[1], w_l.at[q, w])

    def rest_wait(w):
        weight_wait(w, range(4))

    @pl.when(native)
    def _():
        for w in (UP, GATE):
            for copy in across_x(w):
                copy.start()

    gather_start(1)
    for slot in range(SLOTS_GU):
        for copy in wgu_load(slot, slot):
            copy.start()
    for slot in range(SLOTS_D):
        wdn_load(slot, slot).start()

    @pl.when(native)
    def _():
        for w in (UP, GATE, DOWN):
            for copy in own(w):
                copy.start()

    gather_start(2)
    for j in range(1, SRC):
        meta_send(j).wait_recv()

    i16 = lax.broadcasted_iota(jnp.int32, (PEERS, T), 0)
    xe = (x + lax.shift_right_logical(i16, 2)) & 3
    ze = (z + (i16 & 3)) & 3
    expert = (y * 2 + (xe & 1)) * 16 + ze * 4 + lax.shift_right_logical(xe, 1) * 2 + k
    expert = expert.astype(f32)
    before = (
        lax.broadcasted_iota(jnp.int32, (T, T), 0) < lax.broadcasted_iota(jnp.int32, (T, T), 1)
    ).astype(f32).astype(bf16)
    parts = ((0, CUT, 0, RA), (CUT, CAP, RA, ALL))

    def build(s, carry):
        m = mt[s]
        named = jnp.zeros((PEERS, T), f32)
        weight = jnp.zeros((PEERS, T), f32)
        for j in range(4):
            hit = m[j : j + 1, :] == expert
            named = named + jnp.where(hit, 1.0, 0.0)
            weight = weight + jnp.where(hit, m[4 + j : 5 + j, :], 0.0)
        rank = jnp.dot(named.astype(bf16), before, preferred_element_type=f32)
        rank = jnp.where(named > 0.5, rank, -1.0)
        cols = pl.ds(pl.multiple_of(s * T, T), T)
        for s0, s1, r0, r1 in parts:
            q = lax.broadcasted_iota(jnp.int32, ((s1 - s0) * SRC, T), 0)
            q_slot = lax.shift_right_logical(q, 3).astype(f32) + s0
            slot = jnp.where((q & 7) == s, q_slot, -9.0)
            here = rank[:, None, :] == slot[None, :, :]
            pmat[r0:r1, cols] = jnp.where(here, 1.0, 0.0).reshape(r1 - r0, T).astype(bf16)
            scaled = jnp.where(here, weight[:, None, :], 0.0).reshape(r1 - r0, T)
            cmat[cols, r0:r1] = scaled.T.astype(bf16)
        return carry

    lax.fori_loop(0, SRC, build, 0)

    def out_send(c, i, s0, s1, sem):
        slots = pl.ds(s0, s1 - s0)
        return remote(snd.at[c, i, slots], arr.at[c, i, slots], a_s.at[c], sem.at[c], dev(i // 4, 0, i % 4, 0))

    def back_send(n, i, s0, s1, sem):
        slots = pl.ds(s0, s1 - s0)
        return remote(snd.at[n, i, slots], ret.at[n, i, slots], r_s.at[n], sem.at[n], dev(4 - i // 4, 0, 4 - i % 4, 0))

    def swap(c):
        return remote(
            tok.at[c, pl.ds(0, 4)], tok.at[c, pl.ds(4, 4)], b_s.at[c], b_r.at[c], dev(0, 0, 0, 1)
        )

    def put(ref, c, values, which):
        for s0, s1, r0, r1 in which:
            base = which[0][2]
            ref[c, :, s0:s1] = values[r0 - base : r1 - base].reshape(PEERS, s1 - s0, SRC, DC).astype(bf16)

    def put_own(ref, c, values, which):
        for s0, s1, r0, r1 in which:
            base = r0 - which[0][2]
            ref[c, 0, s0:s1] = values[base : base + (s1 - s0) * SRC].reshape(s1 - s0, SRC, DC).astype(bf16)

    def take(ref, c, which):
        for s0, s1, r0, r1 in which:
            stage[r0:r1, :] = ref[c, :, s0:s1].astype(f32).reshape(r1 - r0, DC).astype(bf16)

    def line_wait(c):
        for dy in range(1, 4):
            gather_send(c, dy).wait_recv()
        swap(c).start()

    line_wait(0)
    gather_start(3)

    peers = pl.ds(1, PEERS - 1)

    def expert_dot(slot, r0, r1):
        for h in range(2 * FF // 256):
            cols = slice(h * 256, h * 256 + 256)
            acc[r0:r1, cols] += jnp.dot(stage[r0:r1, :], wgu[slot, :, cols], preferred_element_type=f32)

    def shared_dot(c):
        weights = jnp.concatenate([wsh[j, c].reshape(DC, 128) for j in range(2)], axis=1)
        sacc[...] += jnp.dot(tok[c].reshape(SRC * T, DC), weights, preferred_element_type=f32)

    def forward(it, carry):
        @pl.when(it < NC)
        def _():
            c = it
            swap(c).wait_recv()
            packed = jnp.dot(pmat[...], tok[c].reshape(SRC * T, DC), preferred_element_type=f32)
            put(snd, c, packed, parts)
            put_own(arr, c, packed, parts)

            @pl.when(c < WHOLE_F)
            def _():
                for i in ORDER:
                    out_send(c, i, 0, CAP, a_r).start()

            @pl.when(c >= WHOLE_F)
            def _():
                for i in ORDER:
                    out_send(c, i, 0, CUT, a_r).start()

            @pl.when(c == NC - 1)
            def _():
                def rest(cc, carry):
                    for i in ORDER:
                        out_send(cc, i, CUT, CAP, a_b).start()
                    return carry

                lax.fori_loop(WHOLE_F, NC, rest, 0)

                @pl.when(native)
                def _():
                    for copy in across_x(DOWN):
                        copy.start()

            @pl.when(c + 1 < NC)
            def _():
                line_wait(c + 1)

            @pl.when(c + 4 < NC)
            def _():
                gather_start(c + 4)

        @pl.when(it >= LAG_B)
        def _():
            c = it - LAG_B
            slot = c % SLOTS_GU

            @pl.when(c == LAG_S)
            def _():
                rest_wait(UP)
                rest_wait(GATE)

            @pl.when(c >= LAG_S)
            def _():
                shared_dot(c - LAG_S)

            for copy in wgu_load(c, slot):
                copy.wait()

            @pl.when(c < WHOLE_F)
            def _():
                wait_bytes(arr.at[c, peers], a_r.at[c])
                take(arr, c, parts)
                expert_dot(slot, 0, ALL)

                @pl.when(c + SLOTS_GU < NC)
                def _():
                    for copy in wgu_load(c + SLOTS_GU, slot):
                        copy.start()

            @pl.when(c >= WHOLE_F)
            def _():
                wait_bytes(arr.at[c, peers, pl.ds(0, CUT)], a_r.at[c])
                take(arr, c, parts[:1])
                expert_dot(slot, 0, RA)

        return carry

    lax.fori_loop(0, NC + LAG_B, forward, 0)

    def silu_mul(gate, up):
        return (gate / (1.0 + jnp.exp(-gate)) * up).astype(bf16)

    def activate(r0, r1):
        for h in range(FF // 256):
            cols = slice(h * 256, h * 256 + 256)
            hid[r0:r1, cols] = silu_mul(acc[r0:r1, cols], acc[r0:r1, FF + h * 256 : FF + h * 256 + 256])

    def down(n, which, sem):
        slot = n % SLOTS_D
        done = jnp.dot(hid[which[0][2] : which[-1][3], :], wdn[slot], preferred_element_type=f32)
        put(snd, n, done, which)
        put_own(ret, n, done, which)
        for i in ORDER:
            back_send(n, i, which[0][0], which[-1][1], sem).start()

    activate(0, RA)

    def down_a(n, carry):
        wait_bytes(snd.at[n, peers], a_s.at[n])
        wdn_load(n, n).wait()
        down(n, parts[:1], r_r)
        return carry

    lax.fori_loop(0, SPLIT_R, down_a, 0)
    def shared_rest(c, carry):
        shared_dot(c)
        return carry

    lax.fori_loop(NC - LAG_S, NC, shared_rest, 0)
    shid[...] = silu_mul(sacc[:, 0:128], sacc[:, 128:256])

    def late(c, carry):
        wait_bytes(arr.at[c, peers, pl.ds(CUT, CAP - CUT)], a_b.at[c])
        take(arr, c, parts[1:])
        expert_dot(c % SLOTS_GU, RA, ALL)
        return carry

    lax.fori_loop(WHOLE_F, NC, late, 0)
    activate(RA, ALL)

    def down_b(n, carry):
        down(n, parts[1:], r_b)
        wdn_load(n + SLOTS_D, n).start()
        return carry

    lax.fori_loop(0, SPLIT_R, down_b, 0)

    def part_send(n):
        return remote(psend.at[n % 2], prcv.at[n], p_s.at[n], p_r.at[n], dev(0, 0, 0, 1))

    def line_send(n, dy):
        return remote(
            ysend.at[n % KEEP, dy - 1], yrcv.at[n, 3 - dy], y_s.at[n], y_r.at[n], dev(0, dy, 0, 0)
        )

    half = SRC * T // 2

    def backward(it, carry):
        @pl.when(it < NC)
        def _():
            n = it
            slot = n % SLOTS_D
            wait_bytes(snd.at[n, peers], a_s.at[n])
            wdn_load(n, slot).wait()
            down(n, parts, r_r)

            @pl.when(n + SLOTS_D < NC)
            def _():
                wdn_load(n + SLOTS_D, slot).start()

        @pl.when(jnp.logical_and(it >= LAG_R + 1, it < NC + LAG_R + 1))
        def _():
            n = it - LAG_R - 1

            @pl.when(n >= KEEP)
            def _():
                wait_bytes(ysend.at[n % KEEP], y_s.at[n - KEEP])

            part_send(n).wait_recv()
            for dy in range(1, 4):
                rows = slice(dy * T, dy * T + T)
                ysend[n % KEEP, dy - 1] = (oacc[n % KEEP, rows] + prcv[n, rows].astype(f32)).astype(bf16)
                line_send(n, dy).start()

        @pl.when(it >= LAG_R + 1 + LAG_F)
        def _():
            n = it - LAG_R - 1 - LAG_F
            wait_bytes(yrcv.at[n], y_r.at[n])
            total = oacc[n % KEEP, 0:T] + prcv[n, 0:T].astype(f32)
            for j in range(3):
                total = total + yrcv[n, j].astype(f32)
            out_ref[:, pl.ds(pl.multiple_of(n * DC, DC), DC)] = total.astype(bf16)

        @pl.when(jnp.logical_and(it >= LAG_R, it < NC + LAG_R))
        def _():
            n = it - LAG_R

            @pl.when(n >= 2)
            def _():
                part_send(n - 2).wait_send()

            @pl.when(n < SPLIT_R)
            def _():
                wait_bytes(ret.at[n, peers, pl.ds(0, CUT)], r_r.at[n])
                wait_bytes(ret.at[n, peers, pl.ds(CUT, CAP - CUT)], r_b.at[n])

            @pl.when(n >= SPLIT_R)
            def _():
                wait_bytes(ret.at[n, peers], r_r.at[n])

            take(ret, n, parts)

            @pl.when(n == 0)
            def _():
                rest_wait(DOWN)

            cols = pl.ds(pl.multiple_of(n * DC, DC), DC)
            for lo in (half, 0):
                rows = pl.ds(lo, half)
                part = jnp.dot(cmat[rows, :], stage[...], preferred_element_type=f32)
                part = part + jnp.dot(
                    shid[rows, :], wsd[:, :, cols].reshape(128, DC), preferred_element_type=f32
                )
                if lo:
                    psend[n % 2] = part.astype(bf16)
                    part_send(n).start()
                else:
                    oacc[n % KEEP] = part

        return carry

    lax.fori_loop(SPLIT_R, NC + LAG_R + 1 + LAG_F, backward, 0)

    for j in range(1, SRC):
        meta_send(j).wait_send()

    def drain(c, carry):
        for dy in range(1, 4):
            gather_send(c, dy).wait_send()
        swap(c).wait_send()
        wait_bytes(snd.at[c, peers], r_s.at[c])
        return carry

    lax.fori_loop(0, NC, drain, 0)
    for n in (NC - 2, NC - 1):
        part_send(n).wait_send()
    for n in range(NC - KEEP, NC):
        wait_bytes(ysend.at[n % KEEP], y_s.at[n])

    @pl.when(native)
    def _():
        for w in (UP, GATE, DOWN):
            for copy in across_x(w):
                copy.wait_send()


def per_device(tokens, ids, weights, gate, up, down, sgate, sup, sdown):
    dma = pltpu.SemaphoreType.DMA
    half = SRC * T // 2
    scratch = [
        pltpu.VMEM((NC, SRC, T, DC), bf16),
        pltpu.VMEM((NC, PEERS, CAP, SRC, DC), bf16),
        pltpu.VMEM((NC, PEERS, CAP, SRC, DC), bf16),
        pltpu.VMEM((NC, PEERS, CAP, SRC, DC), bf16),
        pltpu.VMEM((ALL, DC), bf16),
        pltpu.VMEM((ALL, 2 * FF), f32),
        pltpu.VMEM((ALL, FF), bf16),
        pltpu.VMEM((ALL, SRC * T), bf16),
        pltpu.VMEM((SRC * T, ALL), bf16),
        pltpu.VMEM((SLOTS_GU, DC, 2 * FF), bf16),
        pltpu.VMEM((SLOTS_D, FF, DC), bf16),
        pltpu.VMEM((2, NC, 4, DC // 4, 128), bf16),
        pltpu.VMEM((4, 32, D), bf16),
        pltpu.VMEM((SRC * T, 256), f32),
        pltpu.VMEM((SRC * T, 128), bf16),
        pltpu.VMEM((2, half, DC), bf16),
        pltpu.VMEM((NC, half, DC), bf16),
        pltpu.VMEM((KEEP, 3, T, DC), bf16),
        pltpu.VMEM((NC, 3, T, DC), bf16),
        pltpu.VMEM((KEEP, half, DC), f32),
        pltpu.VMEM((SRC, 8, T), f32),
        pltpu.VMEM((4, T), jnp.int32),
        pltpu.VMEM((4, T), f32),
        dma((NC,)),
        dma((NC, 4)),
        dma((NC, 4)),
        dma((NC,)),
        dma((NC,)),
        dma((2,)),
        dma((SRC,)),
        dma((SRC,)),
        dma((NC,)),
        dma((NC,)),
        dma((NC,)),
        dma((NC,)),
        dma((NC,)),
        dma((NC,)),
        dma((4, 3)),
        dma((4, 3)),
        dma((SLOTS_GU, 2)),
        dma((SLOTS_D,)),
        dma((NC,)),
        dma((NC,)),
        dma((NC,)),
        dma((NC,)),
    ]
    hbm = pl.BlockSpec(memory_space=pl.ANY)
    return pl.pallas_call(
        kernel,
        out_shape=jax.ShapeDtypeStruct((T, D), bf16),
        in_specs=[hbm] * 9,
        out_specs=pl.BlockSpec(memory_space=pltpu.VMEM),
        scratch_shapes=scratch,
        cost_estimate=pl.CostEstimate(
            flops=2 * ALL * D * 3 * FF + 2 * SRC * T * D * 3 * 128,
            bytes_accessed=3 * D * FF * 2 + 4 * T * D,
            transcendentals=ALL * FF,
        ),
        compiler_params=pltpu.CompilerParams(
            collective_id=1, has_side_effects=True, vmem_limit_bytes=60 * 2**20
        ),
    )(
        tokens, ids.T, weights.T, gate[0], up[0], down[0],
        sgate.reshape(NC, 4, DC // 4, 128), sup.reshape(NC, 4, DC // 4, 128), sdown.reshape(4, 32, D),
    )


def solution(mesh):
    both = ("row", "col")
    placed = (
        P(both, None),
        P(both, None),
        P(both, None),
        P(both, None, None),
        P(both, None, None),
        P(both, None, None),
        P(None, "row"),
        P(None, "row"),
        P("row", None),
    )
    return jax.shard_map(
        per_device, mesh=mesh, in_specs=placed, out_specs=P(both, None), check_vma=False
    )
```
